32 devices in a mesh: head: 4 (over y, x), inner: 4 (over z), outer: 2 (over core).
Axes of the slice: x: 2, y: 2, z: 4, core: 2. Of those that a mesh axis runs over, the one named last changes fastest.
Arguments:
- queries: bfloat16 [2, 4096, 4096], P('outer', ('head', 'inner')), may hold values from -5 to 5
- key_states: bfloat16 [2, 4096, 4096], P('outer', ('head', 'inner')), may hold values from -5 to 5
- value_states: bfloat16 [2, 4096, 4096], P('outer', ('head', 'inner')), may hold values from -6 to 6
- out_grad: bfloat16 [2, 4096, 4096], P('outer', ('head', 'inner')), may hold values from -6 to 6
- positions: int32 [2, 4096], replicated, may hold values from 0 to 8191, as said below
- doc_start: int32 [2, 4096], replicated, may hold values from 0 to 8191, as said below
Outputs:
- attended: bfloat16 [2, 4096, 4096], P('outer', ('head', 'inner'))
- query_grad: bfloat16 [2, 4096, 4096], P('outer', ('head', 'inner'))
- key_grad: bfloat16 [2, 4096, 4096], P('outer', ('head', 'inner'))
- value_grad: bfloat16 [2, 4096, 4096], P('outer', ('head', 'inner'))
The draws below stay inside these ranges and needn't reach their ends.
Inputs may be any that keep to these rules, and one draw needn't show every extreme that they name: The 8192 positions form 2 * 2 blocks of 2048 consecutive positions; each half of a context rank's 4096 rows holds one whole block in rising order, and which rank and half holds which block varies. The sequence is cut into documents of consecutive positions, each at most 512 positions long and one exactly 512; doc_start is the first position of the token's document.
All inputs are finite; a program needn't handle non-finite values.
Results may differ from the reference program's by a relative error of at most 0.023.
Values may be sent and summed in bfloat16 or wider, within the bound.
A program may use at most 192 MiB of HBM per device.

```python
import jax
import jax.numpy as jnp
from jax import lax

HEADS = 32
DH = 128
ROWS = 4096
DOC_MOST = 512
CTX = 2
TOKENS = 8192
HD = 4096
BLOCK = 512


def span_positions(key):
    half_rows = ROWS // 2
    span_order = jax.random.permutation(key, 2 * CTX).astype(jnp.int32)
    offsets = jnp.arange(half_rows, dtype=jnp.int32)
    return (span_order.reshape(CTX, 2, 1) * half_rows + offsets.reshape(1, 1, half_rows)).reshape(CTX, ROWS)


def draw_positions(key, part):
    return span_positions(key)


def draw_doc_start(key, part):
    token_pos = span_positions(key)
    key = jax.random.fold_in(key, 7)
    shortest = max(DOC_MOST // 4, 1)
    doc_count = TOKENS // shortest + 1
    lengths = jax.random.randint(key, (doc_count,), shortest, DOC_MOST + 1).astype(jnp.int32)
    longest_at = jax.random.randint(jax.random.fold_in(key, 1), (), 0, 4).astype(jnp.int32)
    lengths = jnp.where(jnp.arange(doc_count, dtype=jnp.int32) == longest_at, DOC_MOST, lengths).astype(jnp.int32)
    starts = (jnp.cumsum(lengths) - lengths).astype(jnp.int32)
    is_after = starts.reshape(1, 1, doc_count) <= token_pos[:, :, None]
    return jnp.max(jnp.where(is_after, starts.reshape(1, 1, doc_count), 0), axis=2).astype(jnp.int32)


def draw_queries(key, part):
    key = jax.random.fold_in(key, 3)
    result_rows = jnp.clip(jax.random.normal(key, (CTX, ROWS, HEADS * DH), jnp.float32), -4.0, 4.0)
    return result_rows.astype(jnp.bfloat16)


def draw_key_states(key, part):
    key = jax.random.fold_in(key, 5)
    result_rows = jnp.clip(jax.random.normal(key, (CTX, ROWS, HEADS * DH), jnp.float32), -4.0, 4.0)
    return result_rows.astype(jnp.bfloat16)


def block_levels(key, shape, cuts, least, high):
    factor_of = 1.0
    for dim, parts in cuts:
        draws = jax.random.uniform(jax.random.fold_in(jax.random.fold_in(key, 6), dim), (parts,), jnp.float32, least / len(cuts), high / len(cuts))
        factor_of = factor_of * jnp.repeat(jnp.exp(draws), shape[dim] // parts).reshape((-1,) + (1,) * (len(shape) - 1 - dim))
    return factor_of


def centred(rng, dims, width, limit, shards=(), held_as=jnp.bfloat16):
    values = width * jax.random.normal(rng, dims, jnp.float32)
    if shards:
        values = values * block_levels(rng, dims, shards, -0.22, 0.18)
    return jnp.clip(values, -limit, limit).astype(held_as)


def setup_inputs(seed: int = 0) -> dict:
    key_list = jax.random.split(jax.random.key(seed), 7)
    queries = draw_queries(jax.random.fold_in(key_list[6], 71), 0)
    key_states = draw_key_states(jax.random.fold_in(key_list[6], 71), 0)
    value_states = centred(key_list[2], (CTX, ROWS, HD), 1.0, 6.0, ((0, 2), (1, 16)))
    out_grad = centred(key_list[3], (CTX, ROWS, HD), 1.0, 6.0, ((0, 2), (1, 16)))
    positions = draw_positions(jax.random.fold_in(key_list[6], 71), 0)
    doc_start = draw_doc_start(jax.random.fold_in(key_list[6], 71), 0)
    return dict(queries=queries, key_states=key_states, value_states=value_states, out_grad=out_grad, positions=positions, doc_start=doc_start)


def reference(queries, key_states, value_states, out_grad, positions, doc_start):
    score_scale = DH ** -0.5
    window = DOC_MOST + BLOCK
    where_pos = positions.reshape(TOKENS)
    stored_index = jnp.zeros((TOKENS,), jnp.int32).at[where_pos].set(jnp.arange(TOKENS, dtype=jnp.int32))
    first_sorted = doc_start.reshape(TOKENS)[stored_index]

    def sorted_heads(array):
        return array.reshape(TOKENS, HEADS, DH)[stored_index].transpose(1, 0, 2)

    def single_head(operands):
        query_h, key_h, value_h, grad_h = operands
        padding = jnp.zeros((DOC_MOST, DH), jnp.bfloat16)
        key_padded = jnp.concatenate([padding, key_h], axis=0)
        value_padded = jnp.concatenate([padding, value_h], axis=0)

        def block_step(carried, block_index):
            key_acc, value_acc = carried
            block_start = block_index * BLOCK
            query_block = lax.dynamic_slice_in_dim(query_h, block_start, BLOCK, 0)
            grad_block = lax.dynamic_slice_in_dim(grad_h, block_start, BLOCK, 0)
            key_window = lax.dynamic_slice_in_dim(key_padded, block_start, window, 0)
            value_window = lax.dynamic_slice_in_dim(value_padded, block_start, window, 0)
            query_pos = block_start + jnp.arange(BLOCK, dtype=jnp.int32)
            query_first = lax.dynamic_slice_in_dim(first_sorted, block_start, BLOCK, 0)
            key_pos = block_start - DOC_MOST + jnp.arange(window, dtype=jnp.int32)
            visible = (key_pos[None, :] <= query_pos[:, None]) & (key_pos[None, :] >= query_first[:, None])
            scores = jnp.dot(query_block, key_window.T, preferred_element_type=jnp.float32) * score_scale
            log_total = jax.nn.logsumexp(jnp.where(visible, scores, -jnp.inf), axis=1)
            weights = jnp.where(visible, jnp.exp(scores - log_total[:, None]), 0.0)
            weights_low = weights.astype(jnp.bfloat16)
            attended = jnp.dot(weights_low, value_window, preferred_element_type=jnp.float32).astype(jnp.bfloat16)
            row_delta = jnp.sum(attended.astype(jnp.float32) * grad_block.astype(jnp.float32), axis=1)
            prob_grad = jnp.dot(grad_block, value_window.T, preferred_element_type=jnp.float32)
            score_grad = (weights * (prob_grad - row_delta[:, None]) * score_scale).astype(jnp.bfloat16)
            query_grad = jnp.dot(score_grad, key_window, preferred_element_type=jnp.float32).astype(jnp.bfloat16)
            key_part = jnp.dot(score_grad.T, query_block, preferred_element_type=jnp.float32)
            value_part = jnp.dot(weights_low.T, grad_block, preferred_element_type=jnp.float32)
            key_acc = lax.dynamic_update_slice_in_dim(key_acc, lax.dynamic_slice_in_dim(key_acc, block_start, window, 0) + key_part, block_start, 0)
            value_acc = lax.dynamic_update_slice_in_dim(value_acc, lax.dynamic_slice_in_dim(value_acc, block_start, window, 0) + value_part, block_start, 0)
            return (key_acc, value_acc), (attended, query_grad)

        zero_acc = jnp.zeros((DOC_MOST + TOKENS, DH), jnp.float32)
        (key_acc, value_acc), (attended, query_grad) = lax.scan(block_step, (zero_acc, zero_acc), jnp.arange(TOKENS // BLOCK, dtype=jnp.int32))
        return (attended.reshape(TOKENS, DH), query_grad.reshape(TOKENS, DH), key_acc[DOC_MOST:].astype(jnp.bfloat16), value_acc[DOC_MOST:].astype(jnp.bfloat16))

    results = lax.map(single_head, (sorted_heads(queries), sorted_heads(key_states), sorted_heads(value_states), sorted_heads(out_grad)))

    def back(array):
        return array[:, where_pos].transpose(1, 0, 2).reshape(CTX, ROWS, HEADS * DH)

    return (back(results[0]), back(results[1]), back(results[2]), back(results[3]))
```

```python
import functools

import jax
import jax.numpy as jnp
from jax import lax
from jax.experimental import pallas as pl
from jax.experimental.pallas import tpu as pltpu
from jax.sharding import PartitionSpec as P

DH = 128
DOC_MOST = 512
QUERY_ROWS = 256
SCALE = DH ** (-0.5)
LOG2E = 1.4426950408889634
NEG_LARGE = -1e30
MESH = pl.DeviceIdType.MESH


def dot(a, b, a_dim, b_dim):
    return lax.dot_general(
        a, b, (((a_dim,), (b_dim,)), ((), ())), preferred_element_type=jnp.float32
    )


def wait_bytes(ref, sem):
    pltpu.make_async_copy(ref, ref, sem).wait()


def attend_block(refs, h, half, block, rows):
    qx, gx, kx, vx, first_ref, yout, key_acc, value_acc = refs
    window = DOC_MOST + rows
    low = pl.multiple_of(block * rows, rows)
    half_rows = qx.shape[2]
    q = qx[h, half, pl.ds(low, rows), :]
    g = gx[h, half, pl.ds(low, rows), :]
    k = kx[h, half, pl.ds(low, window), :]
    v = vx[h, half, pl.ds(low, window), :]
    scores = dot(k, q, 1, 1)
    prob_grad = dot(v, g, 1, 1)
    key_row = lax.broadcasted_iota(jnp.int32, (window, rows), 0)
    query_row = lax.broadcasted_iota(jnp.int32, (window, rows), 1)
    visible = (key_row >= first_ref[half, block] - (low - DOC_MOST)) & (
        key_row - query_row <= DOC_MOST
    )
    scores = jnp.where(visible, scores * (SCALE * LOG2E), NEG_LARGE)
    top = jnp.max(scores, axis=0, keepdims=True)
    mass = jnp.exp2(scores - top)
    weights = mass * (1.0 / jnp.sum(mass, axis=0, keepdims=True))
    weights_low = weights.astype(jnp.bfloat16)
    attended = dot(v, weights_low, 0, 0)
    attended_low = attended.astype(jnp.bfloat16).astype(jnp.float32)
    grad_turned = g.astype(jnp.float32).T
    delta = jnp.sum(attended_low * grad_turned, axis=0, keepdims=True)
    score_grad = (weights * (prob_grad - delta)).astype(jnp.bfloat16)
    query_grad = dot(k, score_grad, 0, 0) * SCALE
    out_rows = pl.ds(half * half_rows + low, rows)
    yout[0, h, out_rows, :] = attended.T.astype(jnp.bfloat16)
    yout[1, h, out_rows, :] = query_grad.T.astype(jnp.bfloat16)
    key_acc[half, pl.ds(low, window), :] += dot(score_grad, q, 1, 0)
    value_acc[half, pl.ds(low, window), :] += dot(weights_low, g, 1, 0)


def kernel(
    sizes,
    slots_ref, first_ref, q_hbm, k_hbm, v_hbm, g_hbm,
    o_out, dq_out, dk_out, dv_out,
    qx, kx, vx, gx, tails, stage, parts, yout, key_acc, value_acc,
    in_send, in_recv, tail_send, tail_recv, part_send, part_recv, out_send, out_recv,
):
    inner, group, outer, heads = sizes
    rows = q_hbm.shape[1]
    half_rows = qx.shape[2]
    in_half = group // 2
    me = lax.axis_index("head") * inner + lax.axis_index("inner")
    rank = lax.axis_index("outer")
    query_rows = first_ref.shape[3]
    blocks = half_rows // query_rows

    def peer_of(step):
        return lax.rem(me + step, group)

    def group_id(peer):
        return {"head": peer // inner, "inner": lax.rem(peer, inner)}

    def rank_of(step):
        return lax.rem(rank + step, outer)

    barrier = pltpu.get_barrier_semaphore()

    def greet(step, carry):
        pl.semaphore_signal(barrier, inc=1, device_id=group_id(peer_of(step)), device_id_type=MESH)
        return carry

    lax.fori_loop(1, group, greet, 0)
    for step in range(1, outer):
        pl.semaphore_signal(
            barrier, inc=1, device_id={"outer": rank_of(step)}, device_id_type=MESH
        )
    pl.semaphore_wait(barrier, group - 1 + outer - 1)

    my_half = me // in_half
    my_low = pl.multiple_of(lax.rem(me, in_half) * rows, rows)
    arrays = (
        (k_hbm, kx, DOC_MOST),
        (v_hbm, vx, DOC_MOST),
        (q_hbm, qx, 0),
        (g_hbm, gx, 0),
    )
    outs = (o_out, dq_out, dk_out, dv_out)

    def columns(owner, h):
        return pl.ds(pl.multiple_of((owner * heads + h) * DH, DH), DH)

    for h in range(heads):
        for a, (src, dst, skip) in enumerate(arrays):
            pltpu.make_async_copy(
                src.at[0, :, columns(me, h)],
                dst.at[h, my_half, pl.ds(my_low + skip, rows), :],
                in_recv.at[a, h],
            ).start()

        def send_in(step, carry):
            peer = peer_of(step)
            for a, (src, dst, skip) in enumerate(arrays):
                pltpu.make_async_remote_copy(
                    src_ref=src.at[0, :, columns(peer, h)],
                    dst_ref=dst.at[h, my_half, pl.ds(my_low + skip, rows), :],
                    send_sem=in_send.at[a, h],
                    recv_sem=in_recv.at[a, h],
                    device_id=group_id(peer),
                    device_id_type=MESH,
                ).start()
            return carry

        lax.fori_loop(1, group, send_in, 0)

    def send_out(a, h):
        pltpu.make_async_copy(
            yout.at[a, h, pl.ds(pl.multiple_of(me * rows, rows), rows), :],
            outs[a].at[0, :, columns(me, h)],
            out_recv.at[a],
        ).start()

        def send_one(step, carry):
            peer = peer_of(step)
            pltpu.make_async_remote_copy(
                src_ref=yout.at[a, h, pl.ds(pl.multiple_of(peer * rows, rows), rows), :],
                dst_ref=outs[a].at[0, :, columns(me, h)],
                send_sem=out_send.at[a, h],
                recv_sem=out_recv.at[a],
                device_id=group_id(peer),
                device_id_type=MESH,
            ).start()
            return carry

        lax.fori_loop(1, group, send_one, 0)

    own_slots = pl.ds(2 * rank, 2)
    far_slots = pl.ds(0, 2 * (outer - 1))
    accs = (key_acc, value_acc)
    refs = (qx, gx, kx, vx, first_ref, yout, key_acc, value_acc)
    for h in range(heads):
        for a, (_, dst, skip) in enumerate(arrays):
            wait_bytes(dst.at[h, :, pl.ds(skip, half_rows), :], in_recv.at[a, h])
        for a, ext in enumerate((kx, vx)):
            tail = ext.at[h, :, pl.ds(half_rows, DOC_MOST), :]
            pltpu.make_async_copy(tail, tails[a][h].at[own_slots], tail_recv.at[a, h]).start()
            for step in range(1, outer):
                pltpu.make_async_remote_copy(
                    src_ref=tail,
                    dst_ref=tails[a][h].at[own_slots],
                    send_sem=tail_send.at[a, h],
                    recv_sem=tail_recv.at[a, h],
                    device_id={"outer": rank_of(step)},
                    device_id_type=MESH,
                ).start()
        key_acc[...] = jnp.zeros_like(key_acc)
        value_acc[...] = jnp.zeros_like(value_acc)
        near = min(DOC_MOST // query_rows, blocks)

        def attend(block, carry):
            for half in range(2):
                attend_block(refs, h, half, block, query_rows)
            return carry

        lax.fori_loop(near, blocks, attend, 0)
        for a, ext in enumerate((kx, vx)):
            wait_bytes(tails[a][h], tail_recv.at[a, h])
            for half in range(2):
                ext[h, half, pl.ds(0, DOC_MOST), :] = tails[a][h][slots_ref[half]]
        lax.fori_loop(0, near, attend, 0)
        for a in range(2):
            send_out(a, h)
        for a, acc in enumerate(accs):
            stage[a, h] = acc[:, pl.ds(0, DOC_MOST), :].astype(stage.dtype)
            pltpu.make_async_copy(
                stage.at[a, h], parts[a][h].at[own_slots], part_recv.at[a, h]
            ).start()
            for step in range(1, outer):
                pltpu.make_async_remote_copy(
                    src_ref=stage.at[a, h],
                    dst_ref=parts[a][h].at[own_slots],
                    send_sem=part_send.at[a, h],
                    recv_sem=part_recv.at[a, h],
                    device_id={"outer": rank_of(step)},
                    device_id_type=MESH,
                ).start()
        for a, acc in enumerate(accs):
            factor = SCALE if a == 0 else 1.0
            wait_bytes(parts[a][h], part_recv.at[a, h])
            for half in range(2):
                start = half * half_rows
                bulk = half_rows - DOC_MOST
                part = parts[a][h][slots_ref[2 + half]].astype(jnp.float32)
                part = jnp.where(slots_ref[4 + half] > 0, part, 0.0)
                yout[2 + a, h, pl.ds(start, bulk), :] = (
                    acc[half, pl.ds(DOC_MOST, bulk), :] * factor
                ).astype(jnp.bfloat16)
                yout[2 + a, h, pl.ds(start + bulk, DOC_MOST), :] = (
                    (acc[half, pl.ds(half_rows, DOC_MOST), :] + part) * factor
                ).astype(jnp.bfloat16)
            send_out(2 + a, h)

    others = pl.ds(0, (group - 1) * rows)
    for h in range(heads):
        for a in range(4):
            wait_bytes(yout.at[a, h, others, :], in_send.at[a, h])
            wait_bytes(yout.at[a, h, others, :], out_send.at[a, h])
        if outer > 1:
            for a in range(2):
                wait_bytes(tails[a][h].at[far_slots], tail_send.at[a, h])
                wait_bytes(parts[a][h].at[far_slots], part_send.at[a, h])
    for a in range(4):
        wait_bytes(outs[a], out_recv.at[a])


def slot_of(span_ids, wanted):
    slot_ids = jnp.arange(span_ids.shape[0], dtype=jnp.int32)
    return jnp.sum(jnp.where(span_ids[None, :] == wanted[:, None], slot_ids[None, :], 0), axis=1)


def body(sizes, queries, key_states, value_states, out_grad, positions, doc_start):
    inner, group, outer, heads = sizes
    total_rows = positions.shape[1]
    half_rows = total_rows // 2
    query_rows = min(QUERY_ROWS, half_rows)
    slots = 2 * outer
    pos_table = positions.reshape(slots, half_rows)
    span_ids = pos_table[:, 0] // half_rows
    own_slots = lax.axis_index("outer") * 2 + jnp.arange(2, dtype=jnp.int32)
    span_here = jnp.take(span_ids, own_slots)
    first = jnp.take(doc_start.reshape(slots, half_rows), own_slots, axis=0)
    first = (first - span_here[:, None] * half_rows).reshape(2, half_rows // query_rows, 1, query_rows)
    slot_table = jnp.concatenate(
        [
            slot_of(span_ids, span_here - 1),
            slot_of(span_ids, span_here + 1),
            (span_here + 1 < slots).astype(jnp.int32),
            jnp.zeros((2,), jnp.int32),
        ]
    )
    ext_rows = DOC_MOST + half_rows
    low = jnp.bfloat16
    per_head = [[pltpu.VMEM((slots, DOC_MOST, DH), low)] * heads] * 2
    any_spec = pl.BlockSpec(memory_space=pl.ANY)
    dma = pltpu.SemaphoreType.DMA
    return pl.pallas_call(
        functools.partial(kernel, sizes),
        out_shape=[jax.ShapeDtypeStruct(queries.shape, low)] * 4,
        in_specs=[
            pl.BlockSpec(memory_space=pltpu.SMEM),
            pl.BlockSpec(memory_space=pltpu.VMEM),
        ]
        + [any_spec] * 4,
        out_specs=[any_spec] * 4,
        scratch_shapes=[
            pltpu.VMEM((heads, 2, half_rows, DH), low),
            pltpu.VMEM((heads, 2, ext_rows, DH), low),
            pltpu.VMEM((heads, 2, ext_rows, DH), low),
            pltpu.VMEM((heads, 2, half_rows, DH), low),
            per_head,
            pltpu.VMEM((2, heads, 2, DOC_MOST, DH), low),
            per_head,
            pltpu.VMEM((4, heads, total_rows, DH), low),
            pltpu.VMEM((2, ext_rows, DH), jnp.float32),
            pltpu.VMEM((2, ext_rows, DH), jnp.float32),
            dma((4, heads)),
            dma((4, heads)),
            dma((2, heads)),
            dma((2, heads)),
            dma((2, heads)),
            dma((2, heads)),
            dma((4, heads)),
            dma((4,)),
        ],
        compiler_params=pltpu.CompilerParams(
            collective_id=0, has_side_effects=True, vmem_limit_bytes=56 * 2**20
        ),
    )(slot_table, first, queries, key_states, value_states, out_grad)


def solution(mesh):
    group = mesh.shape["head"] * mesh.shape["inner"]
    outer = mesh.shape["outer"]

    def run(queries, *rest):
        heads = queries.shape[2] // DH // group
        sizes = (mesh.shape["inner"], group, outer, heads)
        spec = P("outer", ("head", "inner"), None)
        return jax.shard_map(
            lambda *args: tuple(body(sizes, *args)),
            mesh=mesh,
            in_specs=(spec, spec, spec, spec, P(), P()),
            out_specs=(spec, spec, spec, spec),
            check_vma=False,
        )(queries, *rest)

    return run
```

```python
import functools

import jax
import jax.numpy as jnp
from jax import lax
from jax.experimental import pallas as pl
from jax.experimental.pallas import tpu as pltpu
from jax.sharding import PartitionSpec as P

DH = 128
DOC_MOST = 512
QUERY_ROWS = 256
SCALE = DH ** (-0.5)
LOG2E = 1.4426950408889634
NEG_LARGE = -1e30
MESH = pl.DeviceIdType.MESH


def dot(a, b, a_dim, b_dim):
    return lax.dot_general(
        a, b, (((a_dim,), (b_dim,)), ((), ())), preferred_element_type=jnp.float32
    )


def wait_bytes(ref, sem):
    pltpu.make_async_copy(ref, ref, sem).wait()


def attend_block(refs, h, half, block, rows, rank, base):
    qx, gx, kx, vx, first_ref, yout, key_acc, value_acc = refs
    window = DOC_MOST + rows
    low = pl.multiple_of(block * rows, rows)
    half_rows = qx.shape[2]
    q = qx[h, half, pl.ds(low, rows), :]
    g = gx[h, half, pl.ds(low, rows), :]
    k = kx[h, half, pl.ds(low, window), :]
    v = vx[h, half, pl.ds(low, window), :]
    scores = dot(k, q, 1, 1)
    prob_grad = dot(v, g, 1, 1)
    key_row = lax.broadcasted_iota(jnp.int32, (window, rows), 0)
    query_row = lax.broadcasted_iota(jnp.int32, (window, rows), 1)
    first = first_ref[pl.ds(rank, 1), pl.ds(pl.multiple_of(half * half_rows + low, rows), rows)]
    visible = (key_row >= first - (base + low - DOC_MOST)) & (
        key_row - query_row <= DOC_MOST
    )
    scores = jnp.where(visible, scores * (SCALE * LOG2E), NEG_LARGE)
    top = jnp.max(scores, axis=0, keepdims=True)
    mass = jnp.exp2(scores - top)
    weights = mass * (1.0 / jnp.sum(mass, axis=0, keepdims=True))
    weights_low = weights.astype(jnp.bfloat16)
    attended = dot(v, weights_low, 0, 0)
    attended_low = attended.astype(jnp.bfloat16).astype(jnp.float32)
    grad_turned = g.astype(jnp.float32).T
    delta = jnp.sum(attended_low * grad_turned, axis=0, keepdims=True)
    score_grad = (weights * (prob_grad - delta)).astype(jnp.bfloat16)
    query_grad = dot(k, score_grad, 0, 0) * SCALE
    out_rows = pl.ds(half * half_rows + low, rows)
    yout[0, h, out_rows, :] = attended.T.astype(jnp.bfloat16)
    yout[1, h, out_rows, :] = query_grad.T.astype(jnp.bfloat16)
    key_acc[half, pl.ds(low, window), :] += dot(score_grad, q, 1, 0)
    value_acc[half, pl.ds(low, window), :] += dot(weights_low, g, 1, 0)


def kernel(
    sizes,
    pos_ref, first_ref, q_hbm, k_hbm, v_hbm, g_hbm,
    o_out, dq_out, dk_out, dv_out,
    qx, kx, vx, gx, tails, stage, parts, yout, key_acc, value_acc,
    in_send, in_recv, tail_send, tail_recv, part_send, part_recv, out_send, out_recv,
):
    inner, group, outer, heads = sizes
    rows = q_hbm.shape[1]
    half_rows = qx.shape[2]
    in_half = group // 2
    me = lax.axis_index("head") * inner + lax.axis_index("inner")
    rank = lax.axis_index("outer")
    query_rows = min(QUERY_ROWS, half_rows)
    blocks = half_rows // query_rows

    def peer_of(step):
        return lax.rem(me + 1 + lax.rem(step - 1 + (group // 2 - 1) * rank, group - 1), group)

    def group_id(peer):
        return {"head": peer // inner, "inner": lax.rem(peer, inner)}

    def rank_of(step):
        return lax.rem(rank + step, outer)

    slots = 2 * outer
    bases = [pos_ref[rank, half * half_rows] for half in range(2)]

    def slot_at(wanted):
        found = jnp.int32(0)
        for slot in range(slots):
            start = pos_ref[slot // 2, (slot % 2) * half_rows]
            found = jnp.where(start == wanted, jnp.int32(slot), found)
        return found

    prev_slots = [slot_at(base - half_rows) for base in bases]
    next_slots = [slot_at(base + half_rows) for base in bases]
    barrier = pltpu.get_barrier_semaphore()

    def greet(step, carry):
        pl.semaphore_signal(barrier, inc=1, device_id=group_id(peer_of(step)), device_id_type=MESH)
        return carry

    lax.fori_loop(1, group, greet, 0)
    for step in range(1, outer):
        pl.semaphore_signal(
            barrier, inc=1, device_id={"outer": rank_of(step)}, device_id_type=MESH
        )
    pl.semaphore_wait(barrier, group - 1 + outer - 1)

    my_half = me // in_half
    my_low = pl.multiple_of(lax.rem(me, in_half) * rows, rows)
    arrays = (
        (k_hbm, kx, DOC_MOST),
        (v_hbm, vx, DOC_MOST),
        (q_hbm, qx, 0),
        (g_hbm, gx, 0),
    )
    outs = (o_out, dq_out, dk_out, dv_out)

    def columns(owner, h):
        return pl.ds(pl.multiple_of((owner * heads + h) * DH, DH), DH)

    for h in range(heads):
        for a, (src, dst, skip) in enumerate(arrays):
            pltpu.make_async_copy(
                src.at[0, :, columns(me, h)],
                dst.at[h, my_half, pl.ds(my_low + skip, rows), :],
                in_recv.at[a, h],
            ).start()

        def send_in(step, carry):
            peer = peer_of(step)
            for a, (src, dst, skip) in enumerate(arrays):
                pltpu.make_async_remote_copy(
                    src_ref=src.at[0, :, columns(peer, h)],
                    dst_ref=dst.at[h, my_half, pl.ds(my_low + skip, rows), :],
                    send_sem=in_send.at[a, h],
                    recv_sem=in_recv.at[a, h],
                    device_id=group_id(peer),
                    device_id_type=MESH,
                ).start()
            return carry

        lax.fori_loop(1, group, send_in, 0)
        if h + 1 < heads:
            for a in range(4):
                wait_bytes(yout.at[a, h, pl.ds(0, (group - 1) * rows), :], in_send.at[a, h])

    def send_out(a, h):
        pltpu.make_async_copy(
            yout.at[a, h, pl.ds(pl.multiple_of(me * rows, rows), rows), :],
            outs[a].at[0, :, columns(me, h)],
            out_recv.at[a],
        ).start()

        def send_one(step, carry):
            peer = peer_of(step)
            pltpu.make_async_remote_copy(
                src_ref=yout.at[a, h, pl.ds(pl.multiple_of(peer * rows, rows), rows), :],
                dst_ref=outs[a].at[0, :, columns(me, h)],
                send_sem=out_send.at[a, h],
                recv_sem=out_recv.at[a],
                device_id=group_id(peer),
                device_id_type=MESH,
            ).start()
            return carry

        lax.fori_loop(1, group, send_one, 0)

    own_slots = pl.ds(2 * rank, 2)
    far_slots = pl.ds(0, 2 * (outer - 1))
    accs = (key_acc, value_acc)
    refs = (qx, gx, kx, vx, first_ref, yout, key_acc, value_acc)
    for h in range(heads):
        for a, (_, dst, skip) in enumerate(arrays):
            wait_bytes(dst.at[h, :, pl.ds(skip, half_rows), :], in_recv.at[a, h])
        for a, ext in enumerate((kx, vx)):
            tail = ext.at[h, :, pl.ds(half_rows, DOC_MOST), :]
            pltpu.make_async_copy(tail, tails[a][h].at[own_slots], tail_recv.at[a, h]).start()
            for step in range(1, outer):
                pltpu.make_async_remote_copy(
                    src_ref=tail,
                    dst_ref=tails[a][h].at[own_slots],
                    send_sem=tail_send.at[a, h],
                    recv_sem=tail_recv.at[a, h],
                    device_id={"outer": rank_of(step)},
                    device_id_type=MESH,
                ).start()
        key_acc[...] = jnp.zeros_like(key_acc)
        value_acc[...] = jnp.zeros_like(value_acc)
        near = min(DOC_MOST // query_rows, blocks)

        def attend(block, carry):
            for half in range(2):
                attend_block(refs, h, half, block, query_rows, rank, bases[half])
            return carry

        lax.fori_loop(near, blocks, attend, 0)
        for a, ext in enumerate((kx, vx)):
            wait_bytes(tails[a][h], tail_recv.at[a, h])
            for half in range(2):
                ext[h, half, pl.ds(0, DOC_MOST), :] = tails[a][h][prev_slots[half]]
        lax.fori_loop(0, near, attend, 0)
        for a in range(2):
            send_out(a, h)
        for a, acc in enumerate(accs):
            stage[a, h] = acc[:, pl.ds(0, DOC_MOST), :].astype(stage.dtype)
            pltpu.make_async_copy(
                stage.at[a, h], parts[a][h].at[own_slots], part_recv.at[a, h]
            ).start()
            for step in range(1, outer):
                pltpu.make_async_remote_copy(
                    src_ref=stage.at[a, h],
                    dst_ref=parts[a][h].at[own_slots],
                    send_sem=part_send.at[a, h],
                    recv_sem=part_recv.at[a, h],
                    device_id={"outer": rank_of(step)},
                    device_id_type=MESH,
                ).start()
        for a, acc in enumerate(accs):
            factor = SCALE if a == 0 else 1.0
            wait_bytes(parts[a][h], part_recv.at[a, h])
            for half in range(2):
                start = half * half_rows
                bulk = half_rows - DOC_MOST
                part = parts[a][h][next_slots[half]].astype(jnp.float32)
                part = jnp.where(bases[half] + half_rows < slots * half_rows, part, 0.0)
                yout[2 + a, h, pl.ds(start, bulk), :] = (
                    acc[half, pl.ds(DOC_MOST, bulk), :] * factor
                ).astype(jnp.bfloat16)
                yout[2 + a, h, pl.ds(start + bulk, DOC_MOST), :] = (
                    (acc[half, pl.ds(half_rows, DOC_MOST), :] + part) * factor
                ).astype(jnp.bfloat16)
            send_out(2 + a, h)

    others = pl.ds(0, (group - 1) * rows)
    for h in range(heads):
        for a in range(4):
            if h + 1 == heads:
                wait_bytes(yout.at[a, h, others, :], in_send.at[a, h])
            wait_bytes(yout.at[a, h, others, :], out_send.at[a, h])
        if outer > 1:
            for a in range(2):
                wait_bytes(tails[a][h].at[far_slots], tail_send.at[a, h])
                wait_bytes(parts[a][h].at[far_slots], part_send.at[a, h])
    for a in range(4):
        wait_bytes(outs[a], out_recv.at[a])


def body(sizes, queries, key_states, value_states, out_grad, positions, doc_start):
    inner, group, outer, heads = sizes
    total_rows = positions.shape[1]
    half_rows = total_rows // 2
    slots = 2 * outer
    ext_rows = DOC_MOST + half_rows
    low = jnp.bfloat16
    per_head = [[pltpu.VMEM((slots, DOC_MOST, DH), low)] * heads] * 2
    any_spec = pl.BlockSpec(memory_space=pl.ANY)
    dma = pltpu.SemaphoreType.DMA
    return pl.pallas_call(
        functools.partial(kernel, sizes),
        out_shape=[jax.ShapeDtypeStruct(queries.shape, low)] * 4,
        in_specs=[
            pl.BlockSpec(memory_space=pltpu.SMEM),
            pl.BlockSpec(memory_space=pltpu.VMEM),
        ]
        + [any_spec] * 4,
        out_specs=[any_spec] * 4,
        scratch_shapes=[
            pltpu.VMEM((heads, 2, half_rows, DH), low),
            pltpu.VMEM((heads, 2, ext_rows, DH), low),
            pltpu.VMEM((heads, 2, ext_rows, DH), low),
            pltpu.VMEM((heads, 2, half_rows, DH), low),
            per_head,
            pltpu.VMEM((2, heads, 2, DOC_MOST, DH), low),
            per_head,
            pltpu.VMEM((4, heads, total_rows, DH), low),
            pltpu.VMEM((2, ext_rows, DH), jnp.float32),
            pltpu.VMEM((2, ext_rows, DH), jnp.float32),
            dma((4, heads)),
            dma((4, heads)),
            dma((2, heads)),
            dma((2, heads)),
            dma((2, heads)),
            dma((2, heads)),
            dma((4, heads)),
            dma((4,)),
        ],
        compiler_params=pltpu.CompilerParams(
            collective_id=0, has_side_effects=True, vmem_limit_bytes=56 * 2**20
        ),
    )(positions, doc_start, queries, key_states, value_states, out_grad)


def solution(mesh):
    group = mesh.shape["head"] * mesh.shape["inner"]
    outer = mesh.shape["outer"]

    def run(queries, *rest):
        heads = queries.shape[2] // DH // group
        sizes = (mesh.shape["inner"], group, outer, heads)
        spec = P("outer", ("head", "inner"), None)
        return jax.shard_map(
            lambda *args: tuple(body(sizes, *args)),
            mesh=mesh,
            in_specs=(spec, spec, spec, spec, P(), P()),
            out_specs=(spec, spec, spec, spec),
            check_vma=False,
        )(queries, *rest)

    return run
```
